512 devices in a mesh: dp: 32 (over x, y), tp: 16 (over z, core).
Axes of the slice: x: 4, y: 8, z: 8, core: 2. Of those that a mesh axis runs over, the one named last changes fastest.
Arguments:
- embeddings: bfloat16 [12288, 192, 256], P(('dp', 'tp')), may hold values from -6 to 6
- projection: bfloat16 [256, 16], replicated, may hold values from -0.375 to 0.375
- compress: bfloat16 [256, 4], replicated, may hold values from -0.375 to 0.375
- w_up: bfloat16 [4096, 4096], P(None, 'tp'), may hold values from -0.09375 to 0.09375
- w_down: bfloat16 [4096, 768], P('tp'), may hold values from -0.125 to 0.125
- output_norm_gain: float32 [1536], P('tp'), may hold values from 0.25 to 1.75
- out_grad: bfloat16 [12288, 1536], P('dp', 'tp'), may hold values from -6 to 6
Outputs:
- block_result: bfloat16 [12288, 1536], P('dp', 'tp')
- grad_down: float32 [4096, 768], P(('tp', 'dp'))
The draws below stay inside these ranges and needn't reach their ends.
All inputs are finite; a program needn't handle non-finite values.
Results may differ from the reference program's by a relative error of at most 0.017.
Values may be sent and summed in bfloat16 or wider, within the bound.
No kernel may reach another device: no remote copies, remote signals or barrier semaphores. Data moves between devices by JAX's collectives and lax.ppermute only.
A program may use at most 64 MiB of HBM per device.

```python
import jax
import jax.numpy as jnp
from jax import lax

FIELDS = 256
EDIM = 192
RANK = 16
HIDDEN_SIZE = 4096
NL = 4
FEAT = 4096
FMW = 768
DOUT = 1536
BATCH = 12288
N_TP = 16


def strengthened(entries, stream_key, source, target, shards_of, factor):
    def block_of(axis_at):
        return (jnp.arange(entries.shape[axis_at]) // (entries.shape[axis_at] // shards_of)).reshape((-1,) + (1,) * (entries.ndim - 1 - axis_at))

    near = jax.random.permutation(stream_key, shards_of)[block_of(target)]
    far = (block_of(target) + shards_of // 2) % shards_of
    return jnp.where((block_of(source) == near) | (block_of(source) == far), factor * entries, entries)


def shard_levels(rng, shape, shards, smallest, largest):
    loudness, own = 1.0, jax.random.fold_in(rng, 6)
    for axis_at, blocks in shards:
        heights = jnp.exp(jax.random.uniform(jax.random.fold_in(own, axis_at), (blocks,), jnp.float32, smallest / len(shards), largest / len(shards)))
        loudness = loudness * jnp.repeat(heights, shape[axis_at] // blocks).reshape([-1 if axis == axis_at else 1 for axis in range(len(shape))])
    return loudness


def gaussian(own_key, shape, deviation, most, split=(), dtype=jnp.bfloat16):
    array = jax.random.normal(own_key, shape, jnp.float32) * deviation
    if len(split) > 0:
        array = shard_levels(own_key, shape, split, -0.22, 0.18) * array
    return jnp.clip(array, min=-most, max=most).astype(dtype)


def bell_draw_with(rng, shape, scale, most, shards, heavy, dtype=jnp.bfloat16):
    values = scale * jax.random.normal(rng, shape, jnp.float32)
    if shards:
        values = values * shard_levels(rng, shape, shards, -0.22, 0.18)
    return jnp.clip(strengthened(values, jax.random.fold_in(rng, 3), *heavy), -most, most).astype(dtype)


def setup_inputs(seed: int = 0) -> dict:
    splits = jax.random.split(jax.random.key(seed), 8)
    embeddings = gaussian(splits[0], (BATCH, EDIM, FIELDS), 1.0, 6.0, ((0, 512),))
    projection = gaussian(splits[1], (FIELDS, RANK), FIELDS ** -0.5, 0.375)
    compress = gaussian(splits[2], (FIELDS, NL), FIELDS ** -0.5, 0.375)
    w_up = gaussian(splits[3], (FEAT, HIDDEN_SIZE), FEAT ** -0.5, 0.09375, ((1, 16),))
    w_down = bell_draw_with(splits[4], (HIDDEN_SIZE, FMW), HIDDEN_SIZE ** -0.5, 0.125, ((0, 16),), (0, 1, 16, 2.0))
    output_norm_gain = jnp.clip(1.0 + 0.15 * jax.random.normal(splits[5], (DOUT,), jnp.float32), 0.25, 1.75)
    out_grad = gaussian(splits[6], (BATCH, DOUT), 1.0, 6.0, ((0, 32), (1, 16)))
    return dict(embeddings=embeddings, projection=projection, compress=compress, w_up=w_up, w_down=w_down, output_norm_gain=output_norm_gain, out_grad=out_grad)


def interact(block, projection, compress):
    x32 = block.astype(jnp.float32)
    pairs = jnp.einsum('sef,fk->sek', x32, projection.astype(jnp.float32)).astype(jnp.bfloat16)
    inter = jnp.einsum('sek,sef->skf', pairs.astype(jnp.float32), x32)
    inter = inter.reshape(block.shape[0], -1)
    center = inter - lax.optimization_barrier(jnp.mean(inter, axis=1, keepdims=True))
    spread = lax.optimization_barrier(jnp.mean(center * center, axis=1, keepdims=True))
    normed = (center / jnp.sqrt(spread + 1e-05)).astype(jnp.bfloat16)
    lcb = jnp.einsum('sef,fj->sje', x32, compress.astype(jnp.float32)).reshape(block.shape[0], -1)
    return (normed, lcb)

def reference(embeddings, projection, compress, w_up, w_down, output_norm_gain, out_grad):
    blocks = embeddings.reshape(-1, 256, embeddings.shape[1], embeddings.shape[2]) if embeddings.shape[0] % 256 == 0 else embeddings.reshape(1, embeddings.shape[0], embeddings.shape[1], embeddings.shape[2])
    normed, lcb = lax.map(lambda b: interact(b, projection, compress), blocks)
    rows = embeddings.shape[0]
    normed = normed.reshape(rows, -1)
    lcb = lcb.reshape(rows, -1)
    hidden = jax.nn.gelu(jnp.dot(normed, w_up, preferred_element_type=jnp.float32), approximate=True).astype(jnp.bfloat16)
    mlp = jnp.dot(hidden, w_down, preferred_element_type=jnp.float32)
    group_mlp = mlp.shape[1] // N_TP
    mixed_rows = jnp.concatenate([mlp.reshape(rows, N_TP, -1), lcb.reshape(rows, N_TP, -1)], axis=2).reshape(rows, -1)
    row_average = lax.optimization_barrier(jnp.mean(mixed_rows, axis=1, keepdims=True))
    var = lax.optimization_barrier(jnp.mean((mixed_rows - row_average) ** 2, axis=1, keepdims=True))
    inverse_deviation = 1.0 / jnp.sqrt(var + 1e-05)
    centered_rows = (mixed_rows - row_average) * inverse_deviation
    block_result = (centered_rows * output_norm_gain).astype(jnp.bfloat16)
    scaled_rows = out_grad.astype(jnp.float32) * output_norm_gain
    first_moment = lax.optimization_barrier(jnp.mean(scaled_rows, axis=1, keepdims=True))
    second_moment = lax.optimization_barrier(jnp.mean(scaled_rows * centered_rows, axis=1, keepdims=True))
    mixed_gradient = ((scaled_rows - first_moment - centered_rows * second_moment) * inverse_deviation).astype(jnp.bfloat16)
    mlp_grad = mixed_gradient.reshape(rows, N_TP, -1)[:, :, :group_mlp].reshape(rows, -1)
    grad_down = jnp.dot(hidden.T, mlp_grad, preferred_element_type=jnp.float32)
    return (block_result, grad_down)
```

```python
import jax
import jax.numpy as jnp
from jax import lax
from jax.sharding import PartitionSpec as P

BF16, F16, F32 = jnp.bfloat16, jnp.float16, jnp.float32
NORMED_SCALE, LCB_SCALE, GG_SCALE = 512.0, 64.0, 4096.0


def high_low(x):
    high = lax.reduce_precision(x, 8, 7)
    return high.astype(BF16), (x - high).astype(BF16)


def on_device(embeddings, projection, compress, w_up, w_down, output_norm_gain, out_grad):
    samples, edim, fields = embeddings.shape
    tp = lax.axis_size("tp")
    dp = lax.axis_size("dp")
    me = lax.axis_index("tp")
    core = me % 2
    group_rows = samples * tp
    feat, fmw = w_up.shape[0], w_down.shape[1]
    own = fmw // tp
    width = 2 * own

    pairs = jnp.einsum("sef,fk->sek", embeddings, projection, preferred_element_type=F32).astype(BF16)
    inter = jnp.einsum("sek,sef->skf", pairs, embeddings, preferred_element_type=F32).reshape(samples, -1)
    center = inter - jnp.mean(inter, axis=1, keepdims=True)
    spread = jnp.mean(center * center, axis=1, keepdims=True)
    normed = (center * (NORMED_SCALE / jnp.sqrt(spread + 1e-05))).astype(F16)
    lcb = jnp.einsum("sef,fj->sje", embeddings, compress, preferred_element_type=F32).reshape(samples, -1)

    gg = out_grad.T.astype(F32) * output_norm_gain[:, None]
    gg_packed = (
        (gg[:own] * GG_SCALE).astype(F16).reshape(3, 2, 8, group_rows).transpose(0, 2, 1, 3).reshape(samples, -1)
    )
    sent = jnp.concatenate([normed, (lcb * LCB_SCALE).astype(F16), gg_packed], axis=1)
    got = lax.all_gather(sent, "tp", axis=0, tiled=True)

    pre = jnp.dot(got[:, :feat].astype(BF16), w_up, preferred_element_type=F32)
    hidden = jax.nn.gelu(pre * (1.0 / NORMED_SCALE), approximate=True).astype(BF16)
    mlp = jnp.einsum("hc,sh->cs", w_down, hidden, preferred_element_type=F32)
    mlp = mlp.reshape(tp // 2, 2, own, group_rows)

    swap = [(i, i ^ 1) for i in range(tp)]
    theirs = lax.dynamic_index_in_dim(mlp, 1 - core, 1, keepdims=False).astype(BF16)
    mine = lax.dynamic_index_in_dim(mlp, core, 1, keepdims=False)
    chip_sum = (mine + lax.ppermute(theirs, "tp", swap).astype(F32)).astype(BF16)
    same_core = [list(range(c, tp, 2)) for c in range(2)]
    arrived = lax.all_to_all(chip_sum, "tp", 0, 0, tiled=True, axis_index_groups=same_core)
    mlp_own = arrived.astype(F32).sum(axis=0)

    lcb_own = lax.dynamic_slice_in_dim(got[:, feat : feat + fmw], me * own, own, 1)
    lcb_own = lcb_own.astype(F32).T * (1.0 / LCB_SCALE)
    mix = jnp.concatenate([mlp_own, lcb_own], axis=0)

    own_mean = jnp.mean(mix, axis=0)
    delta = mix - own_mean
    own_dev = jnp.sum(delta * delta, axis=0)
    own_g = jnp.sum(gg, axis=0)
    own_gd = jnp.sum(gg * delta, axis=0)
    stats = jnp.stack([own_mean, own_dev, own_g, own_gd])
    message = jnp.concatenate([delta[:own].astype(BF16), *high_low(stats)], axis=0)
    every = lax.all_gather(message, "tp", axis=0, tiled=False)

    numbers = every[:, own : own + 4].astype(F32) + every[:, own + 4 :].astype(F32)
    means, devs, gs, gds = (numbers[:, k] for k in range(4))
    full = width * tp
    mean = jnp.mean(means, axis=0)
    shift = means - mean
    var = (jnp.sum(devs, axis=0) + width * jnp.sum(shift * shift, axis=0)) / full
    rstd = 1.0 / jnp.sqrt(var + 1e-05)
    first = jnp.sum(gs, axis=0) / full
    second = jnp.sum(gds + shift * gs, axis=0) * rstd / full

    block = (delta + (own_mean - mean)) * rstd * output_norm_gain[:, None]
    block_result = block.astype(BF16).T

    gg_all = (
        got[:, feat + fmw :].reshape(tp, 3, 8, 2, group_rows).transpose(0, 1, 3, 2, 4).reshape(tp, own, group_rows)
    )
    xhat = (every[:, :own].astype(F32) + shift[:, None]) * rstd
    dmix = ((gg_all.astype(F32) * (1.0 / GG_SCALE) - first - xhat * second) * rstd).astype(BF16)
    dmix = dmix.reshape(fmw, group_rows)
    grad = jnp.einsum("sh,cs->hc", hidden, dmix, preferred_element_type=F32).astype(BF16)
    parts = lax.all_to_all(grad.reshape(dp, -1, fmw), "dp", 0, 0, tiled=True)
    return block_result, parts.astype(F32).sum(axis=0)


def solution(mesh):
    return jax.shard_map(
        on_device,
        mesh=mesh,
        in_specs=(
            P(("dp", "tp"), None, None),
            P(),
            P(),
            P(None, "tp"),
            P("tp", None),
            P("tp"),
            P("dp", "tp"),
        ),
        out_specs=(P("dp", "tp"), P(("tp", "dp"), None)),
        check_vma=False,
    )
```

```python
import jax
import jax.numpy as jnp
from jax import lax
from jax.experimental import pallas as pl
from jax.experimental.pallas import tpu as pltpu
from jax.sharding import PartitionSpec as P

BF16, F16, F32 = jnp.bfloat16, jnp.float16, jnp.float32
NORMED_SCALE, LCB_SCALE, GG_SCALE = 512.0, 64.0, 4096.0
NT = (((1,), (1,)), ((), ()))
MIB = 1 << 20


def call(kernel, out_shape, *operands, flops=0, nbytes=0, vmem=16, **kw):
    return pl.pallas_call(
        kernel,
        out_shape=out_shape,
        compiler_params=pltpu.CompilerParams(vmem_limit_bytes=vmem * MIB),
        cost_estimate=pl.CostEstimate(flops=flops, bytes_accessed=nbytes, transcendentals=0),
        **kw,
    )(*operands)


def column(gain):
    return jnp.broadcast_to(gain, (8, gain.shape[1])).T[:, :1]


def front_kernel(*refs):
    sources, refs = refs[:5], refs[5:]
    out_ref, gg_ref, x_ref, projection_ref, compress_ref, og_ref, gain_ref, inter, lcb, w, sent_ref, sems = refs
    samples, edim, fields = x_ref.shape
    steps, rank, block = inter.shape[:3]
    nl = lcb.shape[1]
    width, rows = gg_ref.shape
    own = width // 2
    copies = [
        pltpu.make_async_copy(source, target, sems.at[k])
        for k, (source, target) in enumerate(
            zip(sources[1:], (projection_ref, compress_ref, og_ref, gain_ref))
        )
    ]
    chunks = [
        pltpu.make_async_copy(
            sources[0].at[pl.ds(r * block, block)], x_ref.at[pl.ds(r * block, block)], sems.at[len(copies) + r]
        )
        for r in range(steps)
    ]
    for copy in copies[:2] + chunks + copies[2:]:
        copy.start()

    w[...] = jnp.zeros_like(w)
    copies[0].wait()
    copies[1].wait()
    w[:rank] = projection_ref[...].astype(F32)
    w[rank : rank + nl] = compress_ref[...].astype(F32)
    start = nl * edim + own * rows // samples
    for r in range(steps):
        chunks[r].wait()
        x = x_ref[r * block : (r + 1) * block]
        both = lax.dot_general(x.reshape(block * edim, fields), w[...].astype(BF16), NT, preferred_element_type=F32)
        for i in range(block):
            turned = both[i * edim : (i + 1) * edim].T
            lcb[r, :, i, :] = turned[rank : rank + nl]
            inter[r, :, i, :] = jnp.dot(turned[:rank].astype(BF16), x[i], preferred_element_type=F32)
        at = slice(r * block, (r + 1) * block)
        lines = [inter[r, k] for k in range(rank)]
        mean = jnp.sum(sum(lines[1:], lines[0]), axis=1, keepdims=True) / (rank * fields)
        lines = [line - mean for line in lines]
        squares = [line * line for line in lines]
        spread = jnp.sum(sum(squares[1:], squares[0]), axis=1, keepdims=True) / (rank * fields)
        factor = NORMED_SCALE / jnp.sqrt(spread + 1e-05)
        for k in range(rank):
            sent_ref[at, start + k * fields : start + (k + 1) * fields] = lines[k] * factor
        for j in range(nl):
            sent_ref[at, j * edim : (j + 1) * edim] = lcb[r, j] * LCB_SCALE

    for copy in copies[2:]:
        copy.wait()
    gg = og_ref[...].astype(F32) * column(gain_ref[...])
    gg_ref[...] = gg
    for k in range(own // 8):
        r, q = divmod(k, 2)
        lane = nl * edim + q * rows
        sent_ref[r * 8 : r * 8 + 8, lane : lane + rows] = gg[k * 8 : k * 8 + 8] * GG_SCALE
    out_ref[...] = sent_ref[...].astype(BF16)


def front(embeddings, projection, compress, out_grad, gain):
    samples, edim, fields = embeddings.shape
    rank, nl, block = projection.shape[1], compress.shape[1], 8
    rows, width = out_grad.shape
    total = nl * edim + (width // 2) * rows // samples + rank * fields
    steps = samples // block
    return call(
        front_kernel,
        (
            jax.ShapeDtypeStruct((samples, total), BF16),
            jax.ShapeDtypeStruct((width, rows), F32),
        ),
        embeddings,
        projection.T,
        compress.T,
        out_grad.T,
        gain.reshape(1, -1),
        flops=2 * samples * edim * fields * 144,
        nbytes=embeddings.size * 2,
        vmem=54,
        in_specs=[pl.BlockSpec(memory_space=pltpu.HBM)] * 5,
        out_specs=(pl.BlockSpec(memory_space=pltpu.VMEM),) * 2,
        scratch_shapes=[
            pltpu.VMEM((samples, edim, fields), BF16),
            pltpu.VMEM((rank, fields), BF16),
            pltpu.VMEM((nl, fields), BF16),
            pltpu.VMEM((width, rows), BF16),
            pltpu.VMEM((1, width), F32),
            pltpu.VMEM((steps, rank, block, fields), F32),
            pltpu.VMEM((steps, nl, block, edim), F32),
            pltpu.VMEM((128, fields), F32),
            pltpu.VMEM((samples, total), F32),
            pltpu.SemaphoreType.DMA((4 + steps,)),
        ],
    )


def down_kernel(place_ref, hidden_ref, w_ref, tail_ref, mine_ref, theirs_ref, lcb_ref, gg_ref, mlp):
    core, me = place_ref[0], place_ref[1]
    chips, own, rows = mine_ref.shape
    fmw = w_ref.shape[1]
    product = lax.dot_general(w_ref[...], hidden_ref[...], (((0,), (1,)), ((), ())), preferred_element_type=F32)
    mlp[...] = product.reshape(mlp.shape)
    for z in range(chips):
        mine_ref[z] = mlp[z, core]
        theirs_ref[z] = mlp[z, 1 - core].astype(BF16)
    lane = lax.broadcasted_iota(jnp.int32, (own, fmw), 1)
    line = lax.broadcasted_iota(jnp.int32, (own, fmw), 0)
    select = jnp.where(lane == line + me * own, 1.0 / LCB_SCALE, 0.0).astype(BF16)
    lcb_ref[...] = lax.dot_general(select, tail_ref[:, :fmw], NT, preferred_element_type=F32)
    for z in range(chips):
        part = tail_ref[z * own : (z + 1) * own, fmw:].astype(F32) * (1.0 / GG_SCALE)
        pieces = [part[r * 8 : r * 8 + 8, q * rows : (q + 1) * rows] for r in range(own // 8) for q in range(2)]
        gg_ref[2 * z * own : 2 * (z + 1) * own] = jnp.concatenate(pieces, axis=0).astype(BF16)


def down(place, hidden, w_down, tail, own):
    rows, fmw = hidden.shape[0], w_down.shape[1]
    chips = fmw // (2 * own)
    vmem = pl.BlockSpec(memory_space=pltpu.VMEM)
    return call(
        down_kernel,
        (
            jax.ShapeDtypeStruct((chips, own, rows), F32),
            jax.ShapeDtypeStruct((chips, own, rows), BF16),
            jax.ShapeDtypeStruct((own, rows), F32),
            jax.ShapeDtypeStruct((fmw, rows), BF16),
        ),
        place,
        hidden,
        w_down,
        tail,
        flops=2 * rows * fmw * w_down.shape[0],
        nbytes=4 * MIB,
        in_specs=[pl.BlockSpec(memory_space=pltpu.SMEM)] + [vmem] * 3,
        out_specs=(vmem,) * 4,
        scratch_shapes=[pltpu.VMEM((chips, 2, own, rows), F32)],
    )


def stats_kernel(arrived_ref, lcb_ref, gg_ref, message_ref, delta_ref):
    own, rows = arrived_ref.shape[1:]
    mlp = arrived_ref[0].astype(F32)
    for z in range(1, arrived_ref.shape[0]):
        mlp = mlp + arrived_ref[z].astype(F32)
    lcb = lcb_ref[...]
    mean = (jnp.sum(mlp, axis=0, keepdims=True) + jnp.sum(lcb, axis=0, keepdims=True)) / (2 * own)
    d0, d1 = mlp - mean, lcb - mean
    g0, g1 = gg_ref[:own], gg_ref[own:]
    dev = jnp.sum(d0 * d0, axis=0, keepdims=True) + jnp.sum(d1 * d1, axis=0, keepdims=True)
    g = jnp.sum(g0, axis=0, keepdims=True) + jnp.sum(g1, axis=0, keepdims=True)
    gd = jnp.sum(g0 * d0, axis=0, keepdims=True) + jnp.sum(g1 * d1, axis=0, keepdims=True)
    stats = jnp.concatenate([mean, dev, g, gd], axis=0)
    high = stats.astype(BF16).astype(F32)
    message_ref[...] = jnp.concatenate([d0, high, stats - high], axis=0).astype(BF16)
    delta_ref[:own], delta_ref[own : 2 * own] = d0, d1
    delta_ref[2 * own :] = jnp.broadcast_to(mean, (8, rows))


def own_stats(arrived, lcb, gg):
    _, own, rows = arrived.shape
    return call(
        stats_kernel,
        (jax.ShapeDtypeStruct((own + 8, rows), BF16), jax.ShapeDtypeStruct((2 * own + 8, rows), F32)),
        arrived,
        lcb,
        gg,
        flops=own * rows * 20,
        nbytes=arrived.size * 2,
        in_specs=[pl.BlockSpec(memory_space=pltpu.VMEM)] * 3,
        out_specs=(pl.BlockSpec(memory_space=pltpu.VMEM),) * 2,
    )


def grad_kernel(every_ref, gg_ref, hidden_ref, delta_ref, gain_ref, grad_ref, block_ref, dmix):
    tp, padded, rows = every_ref.shape
    own = padded - 8
    width = 2 * own
    full = width * tp
    deltas, numbers = [], []
    for t in range(tp):
        part = every_ref[t].astype(F32)
        deltas.append(part[:own])
        numbers.append(part[own : own + 4] + part[own + 4 :])
    mean = sum(n[0:1] for n in numbers) / tp
    shifts = [n[0:1] - mean for n in numbers]
    var = sum(n[1:2] + width * s * s for n, s in zip(numbers, shifts)) / full
    rstd = 1.0 / jnp.sqrt(var + 1e-05)
    first = sum(n[2:3] for n in numbers) / full
    second = sum(n[3:4] + s * n[2:3] for n, s in zip(numbers, shifts)) * rstd / full
    scale = rstd * second
    for t in range(tp):
        offset = first + shifts[t] * scale
        g = gg_ref[t * own : (t + 1) * own].astype(F32)
        dmix[t * own : (t + 1) * own] = ((g - offset - deltas[t] * scale) * rstd).astype(BF16)
    grad_ref[...] = lax.dot_general(
        hidden_ref[...], dmix[...], (((0,), (1,)), ((), ())), preferred_element_type=F32
    ).astype(BF16)
    shift = delta_ref[width : width + 1] - mean
    block_ref[...] = ((delta_ref[:width] + shift) * rstd * column(gain_ref[...])).astype(BF16)


def down_gradient(every, gg, hidden, delta, gain):
    tp, padded, rows = every.shape
    fmw, width = gg.shape[0], 2 * (padded - 8)
    return call(
        grad_kernel,
        (jax.ShapeDtypeStruct((hidden.shape[1], fmw), BF16), jax.ShapeDtypeStruct((width, rows), BF16)),
        every,
        gg,
        hidden,
        delta,
        gain.reshape(1, -1),
        flops=2 * rows * fmw * hidden.shape[1],
        nbytes=3 * MIB,
        in_specs=[pl.BlockSpec(memory_space=pltpu.VMEM)] * 5,
        out_specs=(pl.BlockSpec(memory_space=pltpu.VMEM),) * 2,
        scratch_shapes=[pltpu.VMEM((fmw, rows), BF16)],
    )


def on_device(embeddings, projection, compress, w_up, w_down, output_norm_gain, out_grad):
    tp = lax.axis_size("tp")
    dp = lax.axis_size("dp")
    me = lax.axis_index("tp")
    feat, fmw = w_up.shape[0], w_down.shape[1]
    own = fmw // tp

    sent, gg = front(embeddings, projection, compress, out_grad, output_norm_gain)
    got = lax.all_gather(sent.astype(F16), "tp", axis=0, tiled=True)

    pre = jnp.dot(got[:, 2 * fmw :].astype(BF16), w_up, preferred_element_type=F32)
    hidden = jax.nn.gelu(pre * (1.0 / NORMED_SCALE), approximate=True).astype(BF16)
    tail = got[:, : 2 * fmw].astype(BF16)

    place = jnp.stack([me % 2, me]).astype(jnp.int32)
    mine, theirs, lcb_own, gg_all = down(place, hidden, w_down, tail, own)
    swap = [(i, i ^ 1) for i in range(tp)]
    chip_sum = (mine + lax.ppermute(theirs, "tp", swap).astype(F32)).astype(BF16)
    same_core = [list(range(c, tp, 2)) for c in range(2)]
    arrived = lax.all_to_all(chip_sum, "tp", 0, 0, tiled=True, axis_index_groups=same_core)

    message, delta = own_stats(arrived, lcb_own, gg)
    every = lax.all_gather(message, "tp", axis=0, tiled=False)
    grad, block = down_gradient(every, gg_all, hidden, delta, output_norm_gain)
    parts = lax.all_to_all(grad.reshape(dp, -1, fmw), "dp", 0, 0, tiled=True)
    return block.T, parts.astype(F32).sum(axis=0)


def solution(mesh):
    return jax.shard_map(
        on_device,
        mesh=mesh,
        in_specs=(
            P(("dp", "tp"), None, None),
            P(),
            P(),
            P(None, "tp"),
            P("tp", None),
            P("tp"),
            P("dp", "tp"),
        ),
        out_specs=(P("dp", "tp"), P(("tp", "dp"), None)),
        check_vma=False,
    )
```

```python
import jax
import jax.numpy as jnp
from jax import lax
from jax.experimental import pallas as pl
from jax.experimental.pallas import tpu as pltpu
from jax.sharding import PartitionSpec as P

BF16, F16, F32 = jnp.bfloat16, jnp.float16, jnp.float32
NORMED_SCALE, GG_SCALE = 512.0, 4096.0
NT = (((1,), (1,)), ((), ()))
MIB = 1 << 20


def call(kernel, out_shape, *operands, flops=0, nbytes=0, vmem=16, **kw):
    return pl.pallas_call(
        kernel,
        out_shape=out_shape,
        compiler_params=pltpu.CompilerParams(vmem_limit_bytes=vmem * MIB),
        cost_estimate=pl.CostEstimate(flops=flops, bytes_accessed=nbytes, transcendentals=0),
        **kw,
    )(*operands)


def column(gain):
    return jnp.broadcast_to(gain, (8, gain.shape[1])).T[:, :1]


def front_kernel(*refs):
    sources, refs = refs[:5], refs[5:]
    out_ref, lcb_ref, gg_ref, x_ref, projection_ref, compress_ref, og_ref, gain_ref, inter, lcb, w, sent_ref, sems = refs
    samples, edim, fields = x_ref.shape
    steps, rank, block = inter.shape[:3]
    nl = lcb.shape[1]
    width, rows = gg_ref.shape
    own = width // 2
    copies = [
        pltpu.make_async_copy(source, target, sems.at[k])
        for k, (source, target) in enumerate(
            zip(sources[1:], (projection_ref, compress_ref, og_ref, gain_ref))
        )
    ]
    chunks = [
        pltpu.make_async_copy(
            sources[0].at[pl.ds(r * block, block)], x_ref.at[pl.ds(r * block, block)], sems.at[len(copies) + r]
        )
        for r in range(steps)
    ]
    for copy in copies[:2] + chunks + copies[2:]:
        copy.start()

    w[...] = jnp.zeros_like(w)
    copies[0].wait()
    copies[1].wait()
    w[:rank] = projection_ref[...].astype(F32)
    w[rank : rank + nl] = compress_ref[...].astype(F32)
    start = own * rows // samples
    for r in range(steps):
        chunks[r].wait()
        x = x_ref[r * block : (r + 1) * block]
        both = lax.dot_general(x.reshape(block * edim, fields), w[...].astype(BF16), NT, preferred_element_type=F32)
        for i in range(block):
            turned = both[i * edim : (i + 1) * edim].T
            lcb[r, :, i, :] = turned[rank : rank + nl]
            inter[r, :, i, :] = jnp.dot(turned[:rank].astype(BF16), x[i], preferred_element_type=F32)
        at = slice(r * block, (r + 1) * block)
        lines = [inter[r, k] for k in range(rank)]
        mean = jnp.sum(sum(lines[1:], lines[0]), axis=1, keepdims=True) / (rank * fields)
        lines = [line - mean for line in lines]
        squares = [line * line for line in lines]
        spread = jnp.sum(sum(squares[1:], squares[0]), axis=1, keepdims=True) / (rank * fields)
        factor = NORMED_SCALE / jnp.sqrt(spread + 1e-05)
        for k in range(rank):
            sent_ref[at, start + k * fields : start + (k + 1) * fields] = lines[k] * factor
        for j in range(nl):
            lcb_ref[at, j * edim : (j + 1) * edim] = lcb[r, j]

    for copy in copies[2:]:
        copy.wait()
    gg = og_ref[...].astype(F32) * column(gain_ref[...])
    gg_ref[...] = gg
    for k in range(own // 8):
        r, q = divmod(k, 2)
        sent_ref[r * 8 : r * 8 + 8, q * rows : (q + 1) * rows] = gg[k * 8 : k * 8 + 8] * GG_SCALE
    out_ref[...] = sent_ref[...].astype(BF16)


def front(embeddings, projection, compress, out_grad, gain):
    samples, edim, fields = embeddings.shape
    rank, nl, block = projection.shape[1], compress.shape[1], 8
    rows, width = out_grad.shape
    total = (width // 2) * rows // samples + rank * fields
    steps = samples // block
    return call(
        front_kernel,
        (
            jax.ShapeDtypeStruct((samples, total), BF16),
            jax.ShapeDtypeStruct((samples, nl * edim), F32),
            jax.ShapeDtypeStruct((width, rows), F32),
        ),
        embeddings,
        projection.T,
        compress.T,
        out_grad.T,
        gain.reshape(1, -1),
        flops=2 * samples * edim * fields * 144,
        nbytes=embeddings.size * 2,
        vmem=54,
        in_specs=[pl.BlockSpec(memory_space=pltpu.HBM)] * 5,
        out_specs=(pl.BlockSpec(memory_space=pltpu.VMEM),) * 3,
        scratch_shapes=[
            pltpu.VMEM((samples, edim, fields), BF16),
            pltpu.VMEM((rank, fields), BF16),
            pltpu.VMEM((nl, fields), BF16),
            pltpu.VMEM((width, rows), BF16),
            pltpu.VMEM((1, width), F32),
            pltpu.VMEM((steps, rank, block, fields), F32),
            pltpu.VMEM((steps, nl, block, edim), F32),
            pltpu.VMEM((128, fields), F32),
            pltpu.VMEM((samples, total), F32),
            pltpu.SemaphoreType.DMA((4 + steps,)),
        ],
    )


def down_kernel(place_ref, hidden_ref, w_ref, tail_ref, local_ref, mine_ref, theirs_ref, gg_ref, mlp):
    core, chip = place_ref[0], place_ref[1]
    chips, padded, rows = mine_ref.shape
    own = padded - 8
    samples, fmw = local_ref.shape
    product = lax.dot_general(w_ref[...], hidden_ref[...], (((0,), (1,)), ((), ())), preferred_element_type=F32)
    mlp[:, :, :own] = product.reshape(chips, 2, own, rows)
    turned = local_ref[...].T
    lane = lax.broadcasted_iota(jnp.int32, (samples, rows), 1)
    line = lax.broadcasted_iota(jnp.int32, (samples, rows), 0)
    packed = jnp.zeros((2 * chips * 8, rows), F32)
    for k in range(own // 8):
        lines = [turned[g * own + k * 8 : g * own + k * 8 + 8] for g in range(2 * chips)]
        first = ((k + chip) % chips * 2 + core) * samples
        spot = jnp.where(lane == line + first, 1.0, 0.0).astype(BF16)
        packed += jnp.dot(jnp.concatenate(lines, axis=0).astype(BF16), spot, preferred_element_type=F32)
    mlp[:, :, own:] = packed.reshape(chips, 2, 8, rows)
    for z in range(chips):
        mine_ref[z] = mlp[z, core]
        theirs_ref[z] = mlp[z, 1 - core].astype(BF16)
    for z in range(chips):
        part = tail_ref[z * own : (z + 1) * own].astype(F32) * (1.0 / GG_SCALE)
        pieces = [part[r * 8 : r * 8 + 8, q * rows : (q + 1) * rows] for r in range(own // 8) for q in range(2)]
        gg_ref[2 * z * own : 2 * (z + 1) * own] = jnp.concatenate(pieces, axis=0).astype(BF16)


def down(place, hidden, w_down, tail, local, own):
    rows, fmw = hidden.shape[0], w_down.shape[1]
    chips = fmw // (2 * own)
    vmem = pl.BlockSpec(memory_space=pltpu.VMEM)
    return call(
        down_kernel,
        (
            jax.ShapeDtypeStruct((chips, own + 8, rows), F32),
            jax.ShapeDtypeStruct((chips, own + 8, rows), BF16),
            jax.ShapeDtypeStruct((fmw, rows), BF16),
        ),
        place,
        hidden,
        w_down,
        tail,
        local,
        flops=2 * rows * fmw * w_down.shape[0],
        nbytes=4 * MIB,
        in_specs=[pl.BlockSpec(memory_space=pltpu.SMEM)] + [vmem] * 4,
        out_specs=(vmem,) * 3,
        scratch_shapes=[pltpu.VMEM((chips, 2, own + 8, rows), F32)],
    )


def stats_kernel(arrived_ref, gg_ref, message_ref, delta_ref):
    chips, padded, rows = arrived_ref.shape
    own = padded - 8
    arrived = [arrived_ref[z].astype(F32) for z in range(chips)]
    mlp = sum(a[:own] for a in arrived)
    lane = lax.broadcasted_iota(jnp.int32, (8, rows), 1)
    span = rows // chips
    blocks = [(lane >= span * b) & (lane < span * (b + 1)) for b in range(chips)]
    lines = []
    for k in range(own // 8):
        line = jnp.zeros((8, rows), F32)
        for z in range(chips):
            line = jnp.where(blocks[(k + z) % chips], arrived[z][own:], line)
        lines.append(pltpu.roll(line, (rows - span * k) % rows, 1) if k else line)
    lcb = jnp.concatenate(lines, axis=0)
    mean = (jnp.sum(mlp, axis=0, keepdims=True) + jnp.sum(lcb, axis=0, keepdims=True)) / (2 * own)
    d0, d1 = mlp - mean, lcb - mean
    g0, g1 = gg_ref[:own], gg_ref[own:]
    dev = jnp.sum(d0 * d0, axis=0, keepdims=True) + jnp.sum(d1 * d1, axis=0, keepdims=True)
    g = jnp.sum(g0, axis=0, keepdims=True) + jnp.sum(g1, axis=0, keepdims=True)
    gd = jnp.sum(g0 * d0, axis=0, keepdims=True) + jnp.sum(g1 * d1, axis=0, keepdims=True)
    stats = jnp.concatenate([mean, dev, g, gd], axis=0)
    high = stats.astype(BF16).astype(F32)
    message_ref[...] = jnp.concatenate([d0, high, stats - high], axis=0).astype(BF16)
    delta_ref[:own], delta_ref[own : 2 * own] = d0, d1
    delta_ref[2 * own :] = jnp.broadcast_to(mean, (8, rows))


def own_stats(arrived, gg):
    _, padded, rows = arrived.shape
    own = padded - 8
    return call(
        stats_kernel,
        (jax.ShapeDtypeStruct((own + 8, rows), BF16), jax.ShapeDtypeStruct((2 * own + 8, rows), F32)),
        arrived,
        gg,
        flops=own * rows * 20,
        nbytes=arrived.size * 2,
        in_specs=[pl.BlockSpec(memory_space=pltpu.VMEM)] * 2,
        out_specs=(pl.BlockSpec(memory_space=pltpu.VMEM),) * 2,
    )


def grad_kernel(every_ref, gg_ref, hidden_ref, delta_ref, gain_ref, grad_ref, block_ref, dmix):
    tp, padded, rows = every_ref.shape
    own = padded - 8
    width = 2 * own
    full = width * tp
    deltas, numbers = [], []
    for t in range(tp):
        part = every_ref[t].astype(F32)
        deltas.append(part[:own])
        numbers.append(part[own : own + 4] + part[own + 4 :])
    mean = sum(n[0:1] for n in numbers) / tp
    shifts = [n[0:1] - mean for n in numbers]
    var = sum(n[1:2] + width * s * s for n, s in zip(numbers, shifts)) / full
    rstd = 1.0 / jnp.sqrt(var + 1e-05)
    first = sum(n[2:3] for n in numbers) / full
    second = sum(n[3:4] + s * n[2:3] for n, s in zip(numbers, shifts)) * rstd / full
    scale = rstd * second
    for t in range(tp):
        offset = first + shifts[t] * scale
        g = gg_ref[t * own : (t + 1) * own].astype(F32)
        dmix[t * own : (t + 1) * own] = ((g - offset - deltas[t] * scale) * rstd).astype(BF16)
    grad_ref[...] = lax.dot_general(
        hidden_ref[...], dmix[...], (((0,), (1,)), ((), ())), preferred_element_type=F32
    ).astype(BF16)
    shift = delta_ref[width : width + 1] - mean
    block_ref[...] = ((delta_ref[:width] + shift) * rstd * column(gain_ref[...])).astype(BF16)


def down_gradient(every, gg, hidden, delta, gain):
    tp, padded, rows = every.shape
    fmw, width = gg.shape[0], 2 * (padded - 8)
    return call(
        grad_kernel,
        (jax.ShapeDtypeStruct((hidden.shape[1], fmw), BF16), jax.ShapeDtypeStruct((width, rows), BF16)),
        every,
        gg,
        hidden,
        delta,
        gain.reshape(1, -1),
        flops=2 * rows * fmw * hidden.shape[1],
        nbytes=3 * MIB,
        in_specs=[pl.BlockSpec(memory_space=pltpu.VMEM)] * 5,
        out_specs=(pl.BlockSpec(memory_space=pltpu.VMEM),) * 2,
        scratch_shapes=[pltpu.VMEM((fmw, rows), BF16)],
    )


def on_device(embeddings, projection, compress, w_up, w_down, output_norm_gain, out_grad):
    tp = lax.axis_size("tp")
    dp = lax.axis_size("dp")
    me = lax.axis_index("tp")
    feat, fmw = w_up.shape[0], w_down.shape[1]
    own = fmw // tp

    sent, local, gg = front(embeddings, projection, compress, out_grad, output_norm_gain)
    got = lax.all_gather(sent.astype(F16), "tp", axis=0, tiled=True)

    pre = jnp.dot(got[:, fmw:].astype(BF16), w_up, preferred_element_type=F32)
    hidden = jax.nn.gelu(pre * (1.0 / NORMED_SCALE), approximate=True).astype(BF16)
    tail = got[:, :fmw].astype(BF16)

    place = jnp.stack([me % 2, me // 2]).astype(jnp.int32)
    mine, theirs, gg_all = down(place, hidden, w_down, tail, local, own)
    swap = [(i, i ^ 1) for i in range(tp)]
    chip_sum = (mine + lax.ppermute(theirs, "tp", swap).astype(F32)).astype(BF16)
    same_core = [list(range(c, tp, 2)) for c in range(2)]
    arrived = lax.all_to_all(chip_sum, "tp", 0, 0, tiled=True, axis_index_groups=same_core)

    message, delta = own_stats(arrived, gg)
    every = lax.all_gather(message, "tp", axis=0, tiled=False)
    grad, block = down_gradient(every, gg_all, hidden, delta, output_norm_gain)
    parts = lax.all_to_all(grad.reshape(dp, -1, fmw), "dp", 0, 0, tiled=True)
    return block.T, parts.astype(F32).sum(axis=0)


def solution(mesh):
    return jax.shard_map(
        on_device,
        mesh=mesh,
        in_specs=(
            P(("dp", "tp"), None, None),
            P(),
            P(),
            P(None, "tp"),
            P("tp", None),
            P("tp"),
            P("dp", "tp"),
        ),
        out_specs=(P("dp", "tp"), P(("tp", "dp"), None)),
        check_vma=False,
    )
```

```python
import jax
import jax.numpy as jnp
from jax import lax
from jax.experimental import pallas as pl
from jax.experimental.pallas import tpu as pltpu
from jax.sharding import PartitionSpec as P

BF16, F16, F32 = jnp.bfloat16, jnp.float16, jnp.float32
NORMED_SCALE, GG_SCALE = 512.0, 4096.0
NT = (((1,), (1,)), ((), ()))
MIB = 1 << 20


def call(kernel, out_shape, *operands, flops=0, nbytes=0, vmem=16, **kw):
    return pl.pallas_call(
        kernel,
        out_shape=out_shape,
        compiler_params=pltpu.CompilerParams(vmem_limit_bytes=vmem * MIB),
        cost_estimate=pl.CostEstimate(flops=flops, bytes_accessed=nbytes, transcendentals=0),
        **kw,
    )(*operands)


def column(gain):
    return jnp.broadcast_to(gain, (8, gain.shape[1])).T[:, :1]


def front_kernel(*refs):
    sources, refs = refs[:5], refs[5:]
    out_ref, lcb_ref, gg_ref, x_ref, projection_ref, compress_ref, og_ref, gain_ref, inter, lcb, w, sent_ref, sems = refs
    samples, edim, fields = x_ref.shape
    steps, rank, block = inter.shape[:3]
    nl = lcb.shape[1]
    width, rows = gg_ref.shape
    own = width // 2
    copies = [
        pltpu.make_async_copy(source, target, sems.at[k])
        for k, (source, target) in enumerate(
            zip(sources[1:], (projection_ref, compress_ref, og_ref, gain_ref))
        )
    ]
    chunks = [
        pltpu.make_async_copy(
            sources[0].at[pl.ds(r * block, block)], x_ref.at[pl.ds(r * block, block)], sems.at[len(copies) + r]
        )
        for r in range(steps)
    ]
    for copy in copies[:2] + chunks + copies[2:]:
        copy.start()

    w[...] = jnp.zeros_like(w)
    copies[0].wait()
    copies[1].wait()
    w[:rank] = projection_ref[...].astype(F32)
    w[rank : rank + nl] = compress_ref[...].astype(F32)
    start = own * rows // samples
    for r in range(steps):
        chunks[r].wait()
        x = x_ref[r * block : (r + 1) * block]
        both = lax.dot_general(x.reshape(block * edim, fields), w[...].astype(BF16), NT, preferred_element_type=F32)
        for i in range(block):
            turned = both[i * edim : (i + 1) * edim].T
            lcb[r, :, i, :] = turned[rank : rank + nl]
            inter[r, :, i, :] = jnp.dot(turned[:rank].astype(BF16), x[i], preferred_element_type=F32)
        at = slice(r * block, (r + 1) * block)
        lines = [inter[r, k] for k in range(rank)]
        mean = jnp.sum(sum(lines[1:], lines[0]), axis=1, keepdims=True) / (rank * fields)
        lines = [line - mean for line in lines]
        squares = [line * line for line in lines]
        spread = jnp.sum(sum(squares[1:], squares[0]), axis=1, keepdims=True) / (rank * fields)
        factor = NORMED_SCALE / jnp.sqrt(spread + 1e-05)
        for k in range(rank):
            sent_ref[at, start + k * fields : start + (k + 1) * fields] = lines[k] * factor
        for j in range(nl):
            lcb_ref[at, j * edim : (j + 1) * edim] = lcb[r, j]

    for copy in copies[2:]:
        copy.wait()
    gg = og_ref[...].astype(F32) * column(gain_ref[...])
    gg_ref[...] = gg
    for k in range(own // 8):
        r, q = divmod(k, 2)
        sent_ref[r * 8 : r * 8 + 8, q * rows : (q + 1) * rows] = gg[k * 8 : k * 8 + 8] * GG_SCALE
    out_ref[...] = sent_ref[...].astype(BF16)


def front(embeddings, projection, compress, out_grad, gain):
    samples, edim, fields = embeddings.shape
    rank, nl, block = projection.shape[1], compress.shape[1], 8
    rows, width = out_grad.shape
    total = (width // 2) * rows // samples + rank * fields
    steps = samples // block
    return call(
        front_kernel,
        (
            jax.ShapeDtypeStruct((samples, total), BF16),
            jax.ShapeDtypeStruct((samples, nl * edim), F32),
            jax.ShapeDtypeStruct((width, rows), F32),
        ),
        *(pltpu.with_memory_space_constraint(x, pltpu.HBM) for x in (embeddings, projection.T, compress.T, out_grad.T, gain.reshape(1, -1))),
        flops=2 * samples * edim * fields * 144,
        nbytes=embeddings.size * 2,
        vmem=16,
        in_specs=[pl.BlockSpec(memory_space=pltpu.HBM)] * 5,
        out_specs=(pl.BlockSpec(memory_space=pltpu.VMEM),) * 3,
        scratch_shapes=[
            pltpu.VMEM((samples, edim, fields), BF16),
            pltpu.VMEM((rank, fields), BF16),
            pltpu.VMEM((nl, fields), BF16),
            pltpu.VMEM((width, rows), BF16),
            pltpu.VMEM((1, width), F32),
            pltpu.VMEM((steps, rank, block, fields), F32),
            pltpu.VMEM((steps, nl, block, edim), F32),
            pltpu.VMEM((128, fields), F32),
            pltpu.VMEM((samples, total), F32),
            pltpu.SemaphoreType.DMA((4 + steps,)),
        ],
    )


def down_kernel(hidden_ref, w_ref, tail_ref, local_ref, mine_ref, theirs_ref, gg_ref, mlp):
    me = lax.axis_index("tp")
    core, chip = me % 2, me // 2
    chips, padded, rows = mine_ref.shape
    own = padded - 8
    samples, fmw = local_ref.shape
    product = lax.dot_general(w_ref[...], hidden_ref[...], (((0,), (1,)), ((), ())), preferred_element_type=F32)
    mlp[:, :, :own] = product.reshape(chips, 2, own, rows)
    turned = local_ref[...].T
    lane = lax.broadcasted_iota(jnp.int32, (samples, rows), 1)
    line = lax.broadcasted_iota(jnp.int32, (samples, rows), 0)
    packed = jnp.zeros((2 * chips * 8, rows), F32)
    for k in range(own // 8):
        lines = [turned[g * own + k * 8 : g * own + k * 8 + 8] for g in range(2 * chips)]
        first = ((k + chip) % chips * 2 + core) * samples
        spot = jnp.where(lane == line + first, 1.0, 0.0).astype(BF16)
        packed += jnp.dot(jnp.concatenate(lines, axis=0).astype(BF16), spot, preferred_element_type=F32)
    mlp[:, :, own:] = packed.reshape(chips, 2, 8, rows)
    for z in range(chips):
        mine_ref[z] = mlp[z, core]
        theirs_ref[z] = mlp[z, 1 - core].astype(BF16)
    for z in range(chips):
        part = tail_ref[z * own : (z + 1) * own].astype(F32) * (1.0 / GG_SCALE)
        pieces = [part[r * 8 : r * 8 + 8, q * rows : (q + 1) * rows] for r in range(own // 8) for q in range(2)]
        gg_ref[2 * z * own : 2 * (z + 1) * own] = jnp.concatenate(pieces, axis=0).astype(BF16)


def down(hidden, w_down, tail, local, own):
    rows, fmw = hidden.shape[0], w_down.shape[1]
    chips = fmw // (2 * own)
    vmem = pl.BlockSpec(memory_space=pltpu.VMEM)
    return call(
        down_kernel,
        (
            jax.ShapeDtypeStruct((chips, own + 8, rows), F32),
            jax.ShapeDtypeStruct((chips, own + 8, rows), BF16),
            jax.ShapeDtypeStruct((fmw, rows), BF16),
        ),
        hidden,
        w_down,
        tail,
        local,
        flops=2 * rows * fmw * w_down.shape[0],
        nbytes=4 * MIB,
        in_specs=[vmem] * 4,
        out_specs=(vmem,) * 3,
        scratch_shapes=[pltpu.VMEM((chips, 2, own + 8, rows), F32)],
    )


def join_kernel(mine_ref, both_ref, out_ref):
    other = 1 - lax.axis_index("tp") % 2
    out_ref[...] = (mine_ref[...] + both_ref[other].astype(F32)).astype(BF16)


def join(mine, both):
    vmem = pl.BlockSpec(memory_space=pltpu.VMEM)
    return call(
        join_kernel,
        jax.ShapeDtypeStruct(mine.shape, BF16),
        mine,
        both,
        flops=mine.size,
        nbytes=mine.size * 8,
        in_specs=[vmem, vmem],
        out_specs=vmem,
    )


def stats_kernel(arrived_ref, gg_ref, message_ref, delta_ref):
    chips, padded, rows = arrived_ref.shape
    own = padded - 8
    arrived = [arrived_ref[z].astype(F32) for z in range(chips)]
    mlp = sum(a[:own] for a in arrived)
    lane = lax.broadcasted_iota(jnp.int32, (8, rows), 1)
    span = rows // chips
    blocks = [(lane >= span * b) & (lane < span * (b + 1)) for b in range(chips)]
    lines = []
    for k in range(own // 8):
        line = jnp.zeros((8, rows), F32)
        for z in range(chips):
            line = jnp.where(blocks[(k + z) % chips], arrived[z][own:], line)
        lines.append(pltpu.roll(line, (rows - span * k) % rows, 1) if k else line)
    lcb = jnp.concatenate(lines, axis=0)
    mean = (jnp.sum(mlp, axis=0, keepdims=True) + jnp.sum(lcb, axis=0, keepdims=True)) / (2 * own)
    d0, d1 = mlp - mean, lcb - mean
    g0, g1 = gg_ref[:own], gg_ref[own:]
    dev = jnp.sum(d0 * d0, axis=0, keepdims=True) + jnp.sum(d1 * d1, axis=0, keepdims=True)
    g = jnp.sum(g0, axis=0, keepdims=True) + jnp.sum(g1, axis=0, keepdims=True)
    gd = jnp.sum(g0 * d0, axis=0, keepdims=True) + jnp.sum(g1 * d1, axis=0, keepdims=True)
    stats = jnp.concatenate([mean, dev, g, gd], axis=0)
    high = stats.astype(BF16).astype(F32)
    message_ref[...] = jnp.concatenate([d0, high, stats - high], axis=0).astype(BF16)
    delta_ref[:own], delta_ref[own : 2 * own] = d0, d1
    delta_ref[2 * own :] = jnp.broadcast_to(mean, (8, rows))


def own_stats(arrived, gg):
    _, padded, rows = arrived.shape
    own = padded - 8
    return call(
        stats_kernel,
        (jax.ShapeDtypeStruct((own + 8, rows), BF16), jax.ShapeDtypeStruct((2 * own + 8, rows), F32)),
        arrived,
        gg,
        flops=own * rows * 20,
        nbytes=arrived.size * 2,
        in_specs=[pl.BlockSpec(memory_space=pltpu.VMEM)] * 2,
        out_specs=(pl.BlockSpec(memory_space=pltpu.VMEM),) * 2,
    )


def grad_kernel(every_ref, gg_ref, hidden_ref, delta_ref, gain_ref, grad_ref, block_ref, dmix):
    tp, padded, rows = every_ref.shape
    own = padded - 8
    width = 2 * own
    full = width * tp
    deltas, numbers = [], []
    for t in range(tp):
        part = every_ref[t].astype(F32)
        deltas.append(part[:own])
        numbers.append(part[own : own + 4] + part[own + 4 :])
    mean = sum(n[0:1] for n in numbers) / tp
    shifts = [n[0:1] - mean for n in numbers]
    var = sum(n[1:2] + width * s * s for n, s in zip(numbers, shifts)) / full
    rstd = 1.0 / jnp.sqrt(var + 1e-05)
    first = sum(n[2:3] for n in numbers) / full
    second = sum(n[3:4] + s * n[2:3] for n, s in zip(numbers, shifts)) * rstd / full
    scale = rstd * second
    for t in range(tp):
        offset = first + shifts[t] * scale
        g = gg_ref[t * own : (t + 1) * own].astype(F32)
        dmix[t * own : (t + 1) * own] = ((g - offset - deltas[t] * scale) * rstd).astype(BF16)
    grad_ref[...] = lax.dot_general(
        hidden_ref[...], dmix[...], (((0,), (1,)), ((), ())), preferred_element_type=F32
    ).astype(BF16)
    shift = delta_ref[width : width + 1] - mean
    block_ref[...] = ((delta_ref[:width] + shift) * rstd * column(gain_ref[...])).astype(BF16)


def down_gradient(every, gg, hidden, delta, gain):
    tp, padded, rows = every.shape
    fmw, width = gg.shape[0], 2 * (padded - 8)
    return call(
        grad_kernel,
        (jax.ShapeDtypeStruct((hidden.shape[1], fmw), BF16), jax.ShapeDtypeStruct((width, rows), BF16)),
        every,
        gg,
        hidden,
        delta,
        gain.reshape(1, -1),
        flops=2 * rows * fmw * hidden.shape[1],
        nbytes=3 * MIB,
        in_specs=[pl.BlockSpec(memory_space=pltpu.VMEM)] * 5,
        out_specs=(pl.BlockSpec(memory_space=pltpu.VMEM),) * 2,
        scratch_shapes=[pltpu.VMEM((fmw, rows), BF16)],
    )


def on_device(embeddings, projection, compress, w_up, w_down, output_norm_gain, out_grad):
    tp = lax.axis_size("tp")
    dp = lax.axis_size("dp")
    feat, fmw = w_up.shape[0], w_down.shape[1]
    own = fmw // tp

    sent, local, gg = front(embeddings, projection, compress, out_grad, output_norm_gain)
    got = lax.all_gather(sent.astype(F16), "tp", axis=0, tiled=True)

    pre = jnp.dot(got[:, fmw:].astype(BF16), w_up, preferred_element_type=F32)
    hidden = jax.nn.gelu(pre * (1.0 / NORMED_SCALE), approximate=True).astype(BF16)
    tail = got[:, :fmw].astype(BF16)

    mine, theirs, gg_all = down(hidden, w_down, tail, local, own)
    pairs = [[i, i + 1] for i in range(0, tp, 2)]
    both = lax.all_gather(theirs, "tp", axis=0, tiled=False, axis_index_groups=pairs)
    chip_sum = join(mine, both)
    same_core = [list(range(c, tp, 2)) for c in range(2)]
    arrived = lax.all_to_all(chip_sum, "tp", 0, 0, tiled=True, axis_index_groups=same_core)

    message, delta = own_stats(arrived, gg)
    every = lax.all_gather(message, "tp", axis=0, tiled=False)
    grad, block = down_gradient(every, gg_all, hidden, delta, output_norm_gain)
    parts = lax.all_to_all(grad.reshape(dp, -1, fmw), "dp", 0, 0, tiled=True)
    return block.T, parts.astype(F32).sum(axis=0)


def solution(mesh):
    return jax.shard_map(
        on_device,
        mesh=mesh,
        in_specs=(
            P(("dp", "tp"), None, None),
            P(),
            P(),
            P(None, "tp"),
            P("tp", None),
            P("tp"),
            P("dp", "tp"),
        ),
        out_specs=(P("dp", "tp"), P(("tp", "dp"), None)),
        check_vma=False,
    )
```

```python
import jax
import jax.numpy as jnp
from jax import lax
from jax.experimental import pallas as pl
from jax.experimental.pallas import tpu as pltpu
from jax.sharding import PartitionSpec as P

BF16, F16, F32 = jnp.bfloat16, jnp.float16, jnp.float32
NORMED_SCALE, GG_SCALE = 512.0, 4096.0
NT = (((1,), (1,)), ((), ()))
MIB = 1 << 20


def call(kernel, out_shape, *operands, flops=0, nbytes=0, vmem=16, **kw):
    return pl.pallas_call(
        kernel,
        out_shape=out_shape,
        compiler_params=pltpu.CompilerParams(vmem_limit_bytes=vmem * MIB),
        cost_estimate=pl.CostEstimate(flops=flops, bytes_accessed=nbytes, transcendentals=0),
        **kw,
    )(*operands)


def column(gain):
    return jnp.broadcast_to(gain, (8, gain.shape[1])).T[:, :1]


def front_kernel(*refs):
    sources, refs = refs[:5], refs[5:]
    out_ref, lcb_ref, gg_ref, x_ref, projection_ref, compress_ref, og_ref, gain_ref, inter, lcb, w, sent_ref, sems = refs
    samples, edim, fields = x_ref.shape
    steps, rank, block = inter.shape[:3]
    nl = lcb.shape[1]
    width, rows = gg_ref.shape
    own = width // 2
    copies = [
        pltpu.make_async_copy(source, target, sems.at[k])
        for k, (source, target) in enumerate(
            zip(sources[1:], (projection_ref, compress_ref, og_ref, gain_ref))
        )
    ]
    bounds = ((0, samples // 4), (samples // 4, samples))
    chunks = [
        pltpu.make_async_copy(
            sources[0].at[pl.ds(at, end - at)], x_ref.at[pl.ds(at, end - at)], sems.at[len(copies) + c]
        )
        for c, (at, end) in enumerate(bounds)
    ]
    for copy in copies[:2] + chunks + copies[2:]:
        copy.start()

    w[...] = jnp.zeros_like(w)
    copies[0].wait()
    copies[1].wait()
    w[:rank] = projection_ref[...].astype(F32)
    w[rank : rank + nl] = compress_ref[...].astype(F32)
    start = own * rows // samples
    for c, (at, end) in enumerate(bounds):
        chunks[c].wait()
        if c == 1:
            for copy in copies[2:]:
                copy.wait()
        x = x_ref[at:end]
        both = lax.dot_general(x.reshape(-1, fields), w[...].astype(BF16), NT, preferred_element_type=F32)
        for n in range(end - at):
            r, i = divmod(at + n, block)
            turned = both[n * edim : (n + 1) * edim].T
            lcb[r, :, i, :] = turned[rank : rank + nl]
            inter[r, :, i, :] = jnp.dot(turned[:rank].astype(BF16), x[n], preferred_element_type=F32)
    for r in range(steps):
        at = slice(r * block, (r + 1) * block)
        lines = [inter[r, k] for k in range(rank)]
        mean = jnp.sum(sum(lines[1:], lines[0]), axis=1, keepdims=True) / (rank * fields)
        lines = [line - mean for line in lines]
        squares = [line * line for line in lines]
        spread = jnp.sum(sum(squares[1:], squares[0]), axis=1, keepdims=True) / (rank * fields)
        factor = NORMED_SCALE / jnp.sqrt(spread + 1e-05)
        for k in range(rank):
            sent_ref[at, start + k * fields : start + (k + 1) * fields] = lines[k] * factor
        for j in range(nl):
            lcb_ref[at, j * edim : (j + 1) * edim] = lcb[r, j]

    gg = og_ref[...].astype(F32) * column(gain_ref[...])
    gg_ref[...] = gg
    for k in range(own // 8):
        r, q = divmod(k, 2)
        sent_ref[r * 8 : r * 8 + 8, q * rows : (q + 1) * rows] = gg[k * 8 : k * 8 + 8] * GG_SCALE
    out_ref[...] = sent_ref[...].astype(BF16)


def front(embeddings, projection, compress, out_grad, gain):
    samples, edim, fields = embeddings.shape
    rank, nl, block = projection.shape[1], compress.shape[1], 8
    rows, width = out_grad.shape
    total = (width // 2) * rows // samples + rank * fields
    steps = samples // block
    return call(
        front_kernel,
        (
            jax.ShapeDtypeStruct((samples, total), BF16),
            jax.ShapeDtypeStruct((samples, nl * edim), F32),
            jax.ShapeDtypeStruct((width, rows), F32),
        ),
        *(pltpu.with_memory_space_constraint(x, pltpu.HBM) for x in (embeddings, projection.T, compress.T, out_grad.T, gain.reshape(1, -1))),
        flops=2 * samples * edim * fields * 144,
        nbytes=embeddings.size * 2,
        vmem=16,
        in_specs=[pl.BlockSpec(memory_space=pltpu.HBM)] * 5,
        out_specs=(pl.BlockSpec(memory_space=pltpu.VMEM),) * 3,
        scratch_shapes=[
            pltpu.VMEM((samples, edim, fields), BF16),
            pltpu.VMEM((rank, fields), BF16),
            pltpu.VMEM((nl, fields), BF16),
            pltpu.VMEM((width, rows), BF16),
            pltpu.VMEM((1, width), F32),
            pltpu.VMEM((steps, rank, block, fields), F32),
            pltpu.VMEM((steps, nl, block, edim), F32),
            pltpu.VMEM((128, fields), F32),
            pltpu.VMEM((samples, total), F32),
            pltpu.SemaphoreType.DMA((4 + steps,)),
        ],
    )


def down_kernel(hidden_ref, w_ref, tail_ref, local_ref, mine_ref, theirs_ref, gg_ref, mlp):
    me = lax.axis_index("tp")
    core, chip = me % 2, me // 2
    chips, padded, rows = mine_ref.shape
    own = padded - 8
    samples, fmw = local_ref.shape
    product = lax.dot_general(w_ref[...], hidden_ref[...], (((0,), (1,)), ((), ())), preferred_element_type=F32)
    mlp[:, :, :own] = product.reshape(chips, 2, own, rows)
    turned = local_ref[...].T
    lane = lax.broadcasted_iota(jnp.int32, (samples, rows), 1)
    line = lax.broadcasted_iota(jnp.int32, (samples, rows), 0)
    packed = jnp.zeros((2 * chips * 8, rows), F32)
    for k in range(own // 8):
        lines = [turned[g * own + k * 8 : g * own + k * 8 + 8] for g in range(2 * chips)]
        first = ((k + chip) % chips * 2 + core) * samples
        spot = jnp.where(lane == line + first, 1.0, 0.0).astype(BF16)
        packed += jnp.dot(jnp.concatenate(lines, axis=0).astype(BF16), spot, preferred_element_type=F32)
    mlp[:, :, own:] = packed.reshape(chips, 2, 8, rows)
    for z in range(chips):
        mine_ref[z] = mlp[z, core]
        theirs_ref[z] = mlp[z, 1 - core].astype(BF16)
    for z in range(chips):
        part = tail_ref[z * own : (z + 1) * own].astype(F32) * (1.0 / GG_SCALE)
        pieces = [part[r * 8 : r * 8 + 8, q * rows : (q + 1) * rows] for r in range(own // 8) for q in range(2)]
        gg_ref[2 * z * own : 2 * (z + 1) * own] = jnp.concatenate(pieces, axis=0).astype(BF16)


def down(hidden, w_down, tail, local, own):
    rows, fmw = hidden.shape[0], w_down.shape[1]
    chips = fmw // (2 * own)
    vmem = pl.BlockSpec(memory_space=pltpu.VMEM)
    return call(
        down_kernel,
        (
            jax.ShapeDtypeStruct((chips, own + 8, rows), F32),
            jax.ShapeDtypeStruct((chips, own + 8, rows), BF16),
            jax.ShapeDtypeStruct((fmw, rows), BF16),
        ),
        hidden,
        w_down,
        tail,
        local,
        flops=2 * rows * fmw * w_down.shape[0],
        nbytes=4 * MIB,
        in_specs=[vmem] * 4,
        out_specs=(vmem,) * 3,
        scratch_shapes=[pltpu.VMEM((chips, 2, own + 8, rows), F32)],
    )


def join_kernel(mine_ref, both_ref, out_ref):
    other = 1 - lax.axis_index("tp") % 2
    out_ref[...] = (mine_ref[...] + both_ref[other].astype(F32)).astype(BF16)


def join(mine, both):
    vmem = pl.BlockSpec(memory_space=pltpu.VMEM)
    return call(
        join_kernel,
        jax.ShapeDtypeStruct(mine.shape, BF16),
        mine,
        both,
        flops=mine.size,
        nbytes=mine.size * 8,
        in_specs=[vmem, vmem],
        out_specs=vmem,
    )


def stats_kernel(arrived_ref, gg_ref, message_ref, delta_ref):
    chips, padded, rows = arrived_ref.shape
    own = padded - 8
    arrived = [arrived_ref[z].astype(F32) for z in range(chips)]
    mlp = sum(a[:own] for a in arrived)
    lane = lax.broadcasted_iota(jnp.int32, (8, rows), 1)
    span = rows // chips
    blocks = [(lane >= span * b) & (lane < span * (b + 1)) for b in range(chips)]
    lines = []
    for k in range(own // 8):
        line = jnp.zeros((8, rows), F32)
        for z in range(chips):
            line = jnp.where(blocks[(k + z) % chips], arrived[z][own:], line)
        lines.append(pltpu.roll(line, (rows - span * k) % rows, 1) if k else line)
    lcb = jnp.concatenate(lines, axis=0)
    mean = (jnp.sum(mlp, axis=0, keepdims=True) + jnp.sum(lcb, axis=0, keepdims=True)) / (2 * own)
    d0, d1 = mlp - mean, lcb - mean
    g0, g1 = gg_ref[:own], gg_ref[own:]
    dev = jnp.sum(d0 * d0, axis=0, keepdims=True) + jnp.sum(d1 * d1, axis=0, keepdims=True)
    g = jnp.sum(g0, axis=0, keepdims=True) + jnp.sum(g1, axis=0, keepdims=True)
    gd = jnp.sum(g0 * d0, axis=0, keepdims=True) + jnp.sum(g1 * d1, axis=0, keepdims=True)
    stats = jnp.concatenate([mean, dev, g, gd], axis=0)
    high = stats.astype(BF16).astype(F32)
    message_ref[...] = jnp.concatenate([d0, high, stats - high], axis=0).astype(BF16)
    delta_ref[:own], delta_ref[own : 2 * own] = d0, d1
    delta_ref[2 * own :] = jnp.broadcast_to(mean, (8, rows))


def own_stats(arrived, gg):
    _, padded, rows = arrived.shape
    own = padded - 8
    return call(
        stats_kernel,
        (jax.ShapeDtypeStruct((own + 8, rows), BF16), jax.ShapeDtypeStruct((2 * own + 8, rows), F32)),
        arrived,
        gg,
        flops=own * rows * 20,
        nbytes=arrived.size * 2,
        in_specs=[pl.BlockSpec(memory_space=pltpu.VMEM)] * 2,
        out_specs=(pl.BlockSpec(memory_space=pltpu.VMEM),) * 2,
    )


def grad_kernel(every_ref, gg_ref, hidden_ref, delta_ref, gain_ref, grad_ref, block_ref, dmix, block, sem):
    tp, padded, rows = every_ref.shape
    own = padded - 8
    width = 2 * own
    full = width * tp
    deltas, numbers = [], []
    for t in range(tp):
        part = every_ref[t].astype(F32)
        deltas.append(part[:own])
        numbers.append(part[own : own + 4] + part[own + 4 :])
    mean = sum(n[0:1] for n in numbers) / tp
    shifts = [n[0:1] - mean for n in numbers]
    var = sum(n[1:2] + width * s * s for n, s in zip(numbers, shifts)) / full
    rstd = 1.0 / jnp.sqrt(var + 1e-05)
    first = sum(n[2:3] for n in numbers) / full
    second = sum(n[3:4] + s * n[2:3] for n, s in zip(numbers, shifts)) * rstd / full
    shift = delta_ref[width : width + 1] - mean
    block[...] = ((delta_ref[:width] + shift) * rstd * column(gain_ref[...])).astype(BF16)
    copy = pltpu.make_async_copy(block, block_ref, sem)
    copy.start()
    scale = rstd * second
    for t in range(tp):
        offset = first + shifts[t] * scale
        g = gg_ref[t * own : (t + 1) * own].astype(F32)
        dmix[t * own : (t + 1) * own] = ((g - offset - deltas[t] * scale) * rstd).astype(BF16)
    grad_ref[...] = lax.dot_general(
        hidden_ref[...], dmix[...], (((0,), (1,)), ((), ())), preferred_element_type=F32
    ).astype(BF16)
    copy.wait()


def down_gradient(every, gg, hidden, delta, gain):
    tp, padded, rows = every.shape
    fmw, width = gg.shape[0], 2 * (padded - 8)
    return call(
        grad_kernel,
        (jax.ShapeDtypeStruct((hidden.shape[1], fmw), BF16), jax.ShapeDtypeStruct((width, rows), BF16)),
        every,
        gg,
        hidden,
        delta,
        gain.reshape(1, -1),
        flops=2 * rows * fmw * hidden.shape[1],
        nbytes=3 * MIB,
        in_specs=[pl.BlockSpec(memory_space=pltpu.VMEM)] * 5,
        out_specs=(pl.BlockSpec(memory_space=pltpu.VMEM), pl.BlockSpec(memory_space=pltpu.HBM)),
        scratch_shapes=[
            pltpu.VMEM((fmw, rows), BF16),
            pltpu.VMEM((width, rows), BF16),
            pltpu.SemaphoreType.DMA,
        ],
    )


def on_device(embeddings, projection, compress, w_up, w_down, output_norm_gain, out_grad):
    tp = lax.axis_size("tp")
    dp = lax.axis_size("dp")
    feat, fmw = w_up.shape[0], w_down.shape[1]
    own = fmw // tp

    sent, local, gg = front(embeddings, projection, compress, out_grad, output_norm_gain)
    got = lax.all_gather(sent.astype(F16), "tp", axis=0, tiled=True)

    pre = jnp.dot(got[:, fmw:].astype(BF16), w_up, preferred_element_type=F32)
    hidden = jax.nn.gelu(pre * (1.0 / NORMED_SCALE), approximate=True).astype(BF16)
    tail = got[:, :fmw].astype(BF16)

    mine, theirs, gg_all = down(hidden, w_down, tail, local, own)
    pairs = [[i, i + 1] for i in range(0, tp, 2)]
    both = lax.all_gather(theirs, "tp", axis=0, tiled=False, axis_index_groups=pairs)
    chip_sum = join(mine, both)
    same_core = [list(range(c, tp, 2)) for c in range(2)]
    arrived = lax.all_to_all(chip_sum, "tp", 0, 0, tiled=True, axis_index_groups=same_core)

    message, delta = own_stats(arrived, gg)
    every = lax.all_gather(message, "tp", axis=0, tiled=False)
    grad, block = down_gradient(every, gg_all, hidden, delta, output_norm_gain)
    parts = lax.all_to_all(grad.reshape(dp, -1, fmw), "dp", 0, 0, tiled=True)
    return block.T, parts.astype(F32).sum(axis=0)


def solution(mesh):
    return jax.shard_map(
        on_device,
        mesh=mesh,
        in_specs=(
            P(("dp", "tp"), None, None),
            P(),
            P(),
            P(None, "tp"),
            P("tp", None),
            P("tp"),
            P("dp", "tp"),
        ),
        out_specs=(P("dp", "tp"), P(("tp", "dp"), None)),
        check_vma=False,
    )
```
